256 devices in a mesh: gx: 8 (over y, core), gy: 32 (over z, x).
Axes of the slice: x: 4, y: 4, z: 8, core: 2. Of those that a mesh axis runs over, the one named last changes fastest.
Arguments:
- dual_operators: float32 [16, 32, 1024, 1024], P('gx', 'gy')
- rigid_trace: float32 [16, 32, 6, 1024], P('gx', 'gy'), may hold values from -0.1875 to 0.1875
- coarse_inverse: float32 [8, 32, 12, 3072], P('gx', 'gy'), as said below
- floating: int32 [16, 32], P('gx', 'gy'), may hold values 0 or 1
- block_map: int32 [16, 32, 8], P('gx', 'gy'), may hold values from 0 to 7, each once within a row
- interface_gap: float32 [16, 32, 32, 1024], P('gx', 'gy'), may hold values from -6 to 6
- rigid_load: float32 [16, 32, 6, 32], P('gx', 'gy'), may hold values from -24 to 24
Outputs:
- dual_solution: float32 [16, 32, 32, 1024], P('gx', 'gy')
- dual_residual: float32 [16, 32, 32, 1024], P('gx', 'gy')
The draws below stay inside these ranges and needn't reach their ends.
Inputs may be any that keep to these rules, and one draw needn't show every extreme that they name: coarse_inverse read as a square matrix is exactly symmetric.
All inputs are finite; a program needn't handle non-finite values. No bound on the sum of `floating` on one device may be relied on, other than what follows from the above.
Results may differ from the reference program's by a relative error of at most 0.0003.
Values sent between devices are 32-bit elements; how exact they have to be, the bound alone decides.
No kernel may reach another device: no remote copies, remote signals or barrier semaphores. Data moves between devices by JAX's collectives and lax.ppermute only.
A program may use at most 64 MiB of HBM per device.

```python
import math
import jax
import jax.numpy as jnp
from jax import lax

NL = 1024
R = 32
M = 6
ITERS = 2
SX = 16
SY = 32
NMODES = 3072


def draw_dual_operators(key, part):
    key = jax.random.fold_in(key, 11)
    keys = jax.random.split(key, SX * SY)

    def one_normal(sub_key):
        key_a, key_b = jax.random.split(sub_key)
        noise = jax.random.truncated_normal(key_a, -4.0, 4.0, (NL, NL), jnp.float32)
        diagonal = jnp.exp(jax.random.uniform(key_b, (NL,), jnp.float32, 0.0, math.log(2.0)))
        return (noise + noise.T) * (0.3 / math.sqrt(2.0 * NL)) + jnp.diag(diagonal)
    result = lax.map(one_normal, keys)
    return result.reshape(SX, SY, NL, NL)


def draw_coarse_inverse(key, part):
    key = jax.random.fold_in(key, 23)
    key_a, key_b = jax.random.split(key)
    count = NMODES
    noise = jax.random.truncated_normal(key_a, -4.0, 4.0, (count, count), jnp.float32)
    diagonal = jnp.exp(jax.random.uniform(key_b, (count,), jnp.float32, math.log(0.2), math.log(0.3)))
    full = (noise + noise.T) * (0.075 / math.sqrt(2.0 * count)) + jnp.diag(diagonal)
    return full.reshape(SX // 2, SY, 2 * M, count)


def plant(drawn, own_key, low, high):
    longest = drawn.shape.index(max(drawn.shape))
    spots = []
    for shift in (0, 1):
        where = [jax.random.randint(jax.random.fold_in(own_key, axis), (), 0, length) for axis, length in enumerate(drawn.shape)]
        where[longest] = (where[longest] + shift) % drawn.shape[longest]
        spots.append(tuple(where))
    return drawn.at[spots[0]].set(low).at[spots[1]].set(high)


def levels(own_key, dims, cuts, smallest, high):
    gain, own = 1.0, jax.random.fold_in(own_key, 6)
    for dim, blocks in cuts:
        draws = jnp.exp(jax.random.uniform(jax.random.fold_in(own, dim), (blocks,), jnp.float32, smallest / len(cuts), high / len(cuts)))
        gain = gain * jnp.repeat(draws, dims[dim] // blocks).reshape([-1 if axis == dim else 1 for axis in range(len(dims))])
    return gain


def centred(own_key, dims, scale, bound, cuts=(), kind=jnp.bfloat16):
    factor_of = levels(own_key, dims, cuts, -0.22, 0.18) if cuts else 1.0
    values = jax.random.normal(own_key, dims, jnp.float32) * scale * factor_of
    return jnp.minimum(jnp.maximum(values, -bound), bound).astype(kind)


def setup_inputs(seed: int = 0) -> dict:
    streams_of = jax.random.split(jax.random.key(seed), 8)
    dual_operators = draw_dual_operators(jax.random.fold_in(streams_of[7], 71), 0)
    rigid_trace = centred(streams_of[1], (SX, SY, M, NL), NL ** -0.5, 0.1875, ((0, 8), (1, 32)), jnp.float32)
    coarse_inverse = draw_coarse_inverse(jax.random.fold_in(streams_of[7], 71), 0)
    floating = plant((jax.random.randint(streams_of[3], (SX, SY), 0, 4) < 3).astype(jnp.int32), jax.random.fold_in(streams_of[3], 1), 0, 1)
    block_map = jax.vmap(lambda own: jax.random.permutation(own, 8))(jax.random.split(streams_of[4], SX * SY)).reshape((SX, SY, 8)).astype(jnp.int32)
    interface_gap = centred(streams_of[5], (SX, SY, R, NL), 1.0, 6.0, ((0, 8), (1, 32)), jnp.float32)
    rigid_load = centred(streams_of[6], (SX, SY, M, R), 4.0, 24.0, ((0, 8), (1, 32)), jnp.float32)
    return dict(dual_operators=dual_operators, rigid_trace=rigid_trace, coarse_inverse=coarse_inverse, floating=floating, block_map=block_map, interface_gap=interface_gap, rigid_load=rigid_load)


HI = lax.Precision.HIGHEST

def slot_table(block_map):
    slots = jnp.arange(8, dtype=jnp.int32)
    return (block_map[..., None, :] == slots[:, None]).astype(jnp.float32)

def slot_weights(first, second, sx_all, sy_all):
    first_b, second_b = jnp.broadcast_arrays(first, second)
    outside = jnp.stack([first_b == 0, first_b == sx_all - 1, second_b == 0, second_b == sy_all - 1], -1)
    outside = jnp.repeat(outside, 2, axis=-1)
    return jnp.where(outside, 1.0, 0.5).astype(jnp.float32)

def chol_solve(matrix, right):
    lower = jnp.linalg.cholesky(matrix)
    middle = lax.linalg.triangular_solve(lower, right, left_side=True, lower=True)
    return lax.linalg.triangular_solve(lower, middle, left_side=True, lower=True, transpose_a=True)

def jump_full(field, table):
    sx_all, sy_all, cases, width = field.shape
    blocks = field.reshape(sx_all, sy_all, cases, 8, width // 8)
    slot = jnp.einsum('abqk,abrkc->abrqc', table, blocks, precision=HI)
    zero_x = jnp.zeros_like(slot[:1])
    zero_y = jnp.zeros_like(slot[:, :1])
    lower_x = jnp.concatenate([zero_x, slot[:-1]], 0)[:, :, :, 2:4]
    upper_x = jnp.concatenate([slot[1:], zero_x], 0)[:, :, :, 0:2]
    lower_y = jnp.concatenate([zero_y, slot[:, :-1]], 1)[:, :, :, 6:8]
    upper_y = jnp.concatenate([slot[:, 1:], zero_y], 1)[:, :, :, 4:6]
    partner = jnp.concatenate([lower_x, upper_x, lower_y, upper_y], 3)
    back = jnp.einsum('abqk,abrqc->abrkc', table, slot - partner, precision=HI)
    return back.reshape(sx_all, sy_all, cases, width)

def reference(dual_operators, rigid_trace, coarse_inverse, floating, block_map, interface_gap, rigid_load):
    sx_all, sy_all, modes_sub, width = rigid_trace.shape
    cases = interface_gap.shape[2]
    table = slot_table(block_map)
    omega = slot_weights(jnp.arange(sx_all)[:, None], jnp.arange(sy_all)[None, :], sx_all, sy_all)
    wblock = jnp.einsum('abqk,abq->abk', table, omega, precision=HI)
    wloc = jnp.repeat(wblock, width // 8, axis=-1)
    live = floating.astype(jnp.float32)[:, :, None, None]
    square = coarse_inverse.reshape(coarse_inverse.shape[-1], coarse_inverse.shape[-1])

    def jump(field):
        return jump_full(field, table)

    def inner(left, right):
        return jnp.einsum('abrk,absk->rs', left * wloc[:, :, None, :], right, precision=HI)

    def modes(load):
        vector = load.reshape(sx_all // 2, 2, sy_all, modes_sub, cases).transpose(0, 2, 1, 3, 4).reshape(-1, cases)
        alpha = jnp.dot(square, vector, precision=HI)
        alpha = alpha.reshape(sx_all // 2, sy_all, 2, modes_sub, cases).transpose(0, 2, 1, 3, 4)
        return alpha.reshape(sx_all, sy_all, modes_sub, cases) * live

    def spread(alpha):
        return jump(jnp.einsum('abmr,abmk->abrk', alpha, rigid_trace, precision=HI))

    def project(field):
        load = jnp.einsum('abmk,abrk->abmr', rigid_trace, field, precision=HI) * live
        return field - spread(modes(load))

    def applied(field):
        return jnp.einsum('abrk,abkj->abrj', field, dual_operators, precision=HI)

    def combine(field, mixing):
        return jnp.einsum('abrk,rs->absk', field, mixing, precision=HI)
    solution = spread(modes(rigid_load * live))
    resid = project(jump(interface_gap - applied(solution)))
    direction = resid
    for step in range(ITERS):
        moved = project(direction)
        image = project(jump(applied(moved)))
        curvature = inner(direction, image)
        drive = inner(direction, resid)
        step_len = chol_solve(curvature, drive)
        solution = solution + combine(moved, step_len)
        resid = resid - combine(image, step_len)
        if step + 1 < ITERS:
            coupling = chol_solve(curvature, inner(image, resid))
            direction = resid - combine(direction, coupling)
    return (solution, resid)
```

```python
import jax
import jax.numpy as jnp
from jax import lax
from jax.sharding import PartitionSpec as P


HI = lax.Precision.HIGHEST


def shifted(value, axis, steps):
    count = lax.axis_size(axis)
    initial, last = (max(0, -steps), min(count, count - steps))
    return lax.ppermute(value, axis, [(source, source + steps) for source in range(initial, last)])


def slot_table(block_map):
    slots = jnp.arange(8, dtype=jnp.int32)
    return (block_map[..., None, :] == slots[:, None]).astype(jnp.float32)


def slot_weights(first, second, sx_all, sy_all):
    first_b, second_b = jnp.broadcast_arrays(first, second)
    outside = jnp.stack(
        [first_b == 0, first_b == sx_all - 1, second_b == 0, second_b == sy_all - 1], -1
    )
    outside = jnp.repeat(outside, 2, axis=-1)
    return jnp.where(outside, 1.0, 0.5).astype(jnp.float32)


def chol_solve(matrix, right):
    lower = jnp.linalg.cholesky(matrix)
    middle = lax.linalg.triangular_solve(lower, right, left_side=True, lower=True)
    return lax.linalg.triangular_solve(lower, middle, left_side=True, lower=True, transpose_a=True)


def spread_out(value, axis):
    count = lax.axis_size(axis)
    copies = jnp.broadcast_to(value, (count,) + value.shape)
    return lax.all_to_all(copies, axis, 0, 0, tiled=False)


def gather(rows):
    across = spread_out(rows, "gy")
    return spread_out(across.reshape(-1, 128), "gx").reshape(-1, 128)


def gather_and_sum(rows, sums):
    count = rows.shape[0]
    both = spread_out(jnp.concatenate([rows, sums], 0), "gy")
    part = both[:, :count].reshape(-1, 128)
    both = spread_out(jnp.concatenate([part, both[:, count:].sum(0)], 0), "gx")
    return both[:, : part.shape[0]].reshape(-1, 128), both[:, part.shape[0] :].sum(0)


def per_device(
    dual_operators, rigid_trace, coarse_inverse, floating, block_map, interface_gap, rigid_load
):
    count_x = lax.axis_size("gx")
    count_y = lax.axis_size("gy")
    place_x = lax.axis_index("gx")
    place_y = lax.axis_index("gy")
    table = slot_table(block_map)
    first = 2 * place_x + jnp.arange(2, dtype=jnp.int32)[:, None]
    second = jnp.full((1, 1), place_y, jnp.int32)
    omega = slot_weights(first, second, 2 * count_x, count_y)
    wblock = jnp.einsum("abqk,abq->abk", table, omega, precision=HI)
    wloc = jnp.repeat(wblock, rigid_trace.shape[3] // 8, axis=-1)
    live = floating.astype(jnp.float32)[:, :, None, None]
    own, wide = coarse_inverse.shape[2], coarse_inverse.shape[3]
    fold = coarse_inverse.reshape(own, wide // 4, 4).transpose(2, 0, 1).reshape(4 * own, wide // 4)

    def jump(field):
        subs, cols, width_cases, width = field.shape
        blocks = field.reshape(subs, cols, width_cases, 8, width // 8)
        slot = jnp.einsum("abqk,abrkc->abrqc", table, blocks, precision=HI)
        from_below = shifted(slot[1:2, :, :, 2:4], "gx", 1)
        from_above = shifted(slot[0:1, :, :, 0:2], "gx", -1)
        lower_y = shifted(slot[:, :, :, 6:8], "gy", 1)
        upper_y = shifted(slot[:, :, :, 4:6], "gy", -1)
        lower_x = jnp.concatenate([from_below, slot[0:1, :, :, 2:4]], 0)
        upper_x = jnp.concatenate([slot[1:2, :, :, 0:2], from_above], 0)
        partner = jnp.concatenate([lower_x, upper_x, lower_y, upper_y], 3)
        back = jnp.einsum("abqk,abrqc->abrkc", table, slot - partner, precision=HI)
        return back.reshape(subs, cols, width_cases, width)

    def inner(left, right):
        return jnp.einsum("abrk,absk->rs", left * wloc[:, :, None, :], right, precision=HI)

    def loads(field):
        load = jnp.einsum("abmk,abrk->abmr", rigid_trace, field, precision=HI) * live
        return load.reshape(-1, 128)

    def modes(gathered):
        product = jnp.dot(fold, gathered, precision=HI).reshape(4, own, 4, 32)
        alpha = sum(product[q, :, q] for q in range(4))
        return alpha.reshape(2, 1, -1, 32) * live

    def spread(alpha):
        return jump(jnp.einsum("abmr,abmk->abrk", alpha, rigid_trace, precision=HI))

    def applied(field):
        return jnp.einsum("abrk,abkj->abrj", field, dual_operators, precision=HI)

    def combine(field, mixing):
        return jnp.einsum("abrk,rs->absk", field, mixing, precision=HI)

    def plain(left, right):
        return jnp.einsum("abrk,absk->rs", left, right, precision=HI)

    def packed(*grams):
        return jnp.concatenate([gram.reshape(-1, 128) for gram in grams], 0)

    start = modes(gather((rigid_load * live).reshape(-1, 128)))
    first_solution = spread(start)
    force = jump(interface_gap - applied(first_solution))
    resid = force - spread(modes(gather(loads(force))))
    alpha = modes(gather(loads(resid)))
    moved = resid - spread(alpha)
    pushed = applied(moved)
    hit = jump(pushed)
    gathered, grams = gather_and_sum(
        loads(hit), packed(plain(moved, pushed), inner(resid, resid))
    )
    curvature, drive = grams.reshape(2, 32, 32)
    image = hit - spread(modes(gathered))
    step_len = chol_solve(curvature, drive)
    next_resid = resid - combine(image, step_len)
    gathered, grams = gather_and_sum(loads(image), packed(inner(image, next_resid)))
    coupling = chol_solve(curvature, grams.reshape(32, 32))
    direction = next_resid - combine(resid, coupling)
    mix = jnp.eye(32, dtype=jnp.float32) - coupling
    next_alpha = jnp.einsum("abmr,rs->abms", alpha, mix, precision=HI) - jnp.einsum(
        "abmr,rs->abms", modes(gathered), step_len, precision=HI
    )
    next_moved = direction - spread(next_alpha)
    pushed = applied(next_moved)
    hit = jump(pushed)
    gathered, grams = gather_and_sum(
        loads(hit), packed(plain(next_moved, pushed), inner(direction, next_resid))
    )
    curvature, drive = grams.reshape(2, 32, 32)
    image = hit - spread(modes(gathered))
    next_step = chol_solve(curvature, drive)
    solution = first_solution + combine(moved, step_len) + combine(next_moved, next_step)
    return (solution, next_resid - combine(image, next_step))


def solution(mesh):
    return jax.shard_map(
        per_device,
        mesh=mesh,
        in_specs=(
            P("gx", "gy", None, None),
            P("gx", "gy", None, None),
            P("gx", "gy", None, None),
            P("gx", "gy"),
            P("gx", "gy", None),
            P("gx", "gy", None, None),
            P("gx", "gy", None, None),
        ),
        out_specs=(P("gx", "gy", None, None), P("gx", "gy", None, None)),
        check_vma=False,
    )
```

```python
import jax
import jax.numpy as jnp
from jax import lax
from jax.sharding import Mesh, PartitionSpec as P


HI = lax.Precision.HIGHEST
ALONG = ("y", "core")


def shifted(value, axis, steps):
    count = lax.axis_size(axis)
    initial, last = (max(0, -steps), min(count, count - steps))
    return lax.ppermute(value, axis, [(source, source + steps) for source in range(initial, last)])


def other_core(value):
    return lax.ppermute(value, "core", [(0, 1), (1, 0)])


def slot_table(block_map):
    slots = jnp.arange(8, dtype=jnp.int32)
    return (block_map[..., None, :] == slots[:, None]).astype(jnp.float32)


def slot_weights(first, second, sx_all, sy_all):
    first_b, second_b = jnp.broadcast_arrays(first, second)
    outside = jnp.stack(
        [first_b == 0, first_b == sx_all - 1, second_b == 0, second_b == sy_all - 1], -1
    )
    outside = jnp.repeat(outside, 2, axis=-1)
    return jnp.where(outside, 1.0, 0.5).astype(jnp.float32)


def chol_solve(matrix, right):
    lower = jnp.linalg.cholesky(matrix)
    middle = lax.linalg.triangular_solve(lower, right, left_side=True, lower=True)
    return lax.linalg.triangular_solve(lower, middle, left_side=True, lower=True, transpose_a=True)


def spread_out(value, axis):
    count = lax.axis_size(axis)
    copies = jnp.broadcast_to(value, (count,) + value.shape)
    return lax.all_to_all(copies, axis, 0, 0, tiled=False)


def gather(rows):
    return spread_out(rows.reshape(1, -1), ("y", "gy")).reshape(-1, 128)


def gather_and_sum(rows, sums):
    rows = rows.reshape(-1, 128)
    count = rows.shape[0]
    both = spread_out(jnp.concatenate([rows, sums], 0), "gy")
    part = both[:, :count].reshape(-1, 128)
    both = jnp.concatenate([part, both[:, count:].sum(0)], 0)
    size = lax.axis_size("y")
    pieces = [both] + [
        lax.ppermute(both, "y", [(i, (i + s) % size) for i in range(size)]) for s in range(1, size)
    ]
    total = sum(piece[part.shape[0] :] for piece in pieces)
    order = [piece[: part.shape[0]] for piece in pieces[::-1]]
    ring = jnp.concatenate(order + order[:-1], 0)
    place = (size - 1 - lax.axis_index("y")) * part.shape[0]
    return lax.dynamic_slice_in_dim(ring, place, size * part.shape[0], 0), total


def per_device(
    dual_operators, rigid_trace, coarse_inverse, floating, block_map, interface_gap, rigid_load
):
    count_x = lax.axis_size("y") * lax.axis_size("core")
    count_y = lax.axis_size("gy")
    core = lax.axis_index("core")
    place_x = lax.axis_index("y") * lax.axis_size("core") + core
    place_y = lax.axis_index("gy")
    dual = dual_operators[:, 0]
    trace = rigid_trace[:, 0]
    gap = interface_gap[:, 0]
    modes, width = trace.shape[1:]
    cases = gap.shape[1]
    table = slot_table(block_map[:, 0])
    first = 2 * place_x + jnp.arange(2, dtype=jnp.int32)[:, None]
    second = jnp.full((1, 1), place_y, jnp.int32)
    omega = slot_weights(first, second, 2 * count_x, count_y)[:, 0]
    wblock = jnp.einsum("sqk,sq->sk", table, omega, precision=HI)
    wloc = jnp.repeat(wblock, width // 8, axis=-1)[:, None, :]
    side = jnp.repeat(block_map[:, 0] // 2, width // 8, axis=-1)
    live = floating[:, 0].astype(jnp.float32)[:, None, None]

    def partner(field):
        subs, rows, wide = field.shape
        blocks = field.reshape(subs, rows, 8, wide // 8)
        slot = jnp.einsum("sqk,srkc->srqc", table, blocks, precision=HI)
        from_below = shifted(slot[1:2, :, 2:4], ALONG, 1)
        from_above = shifted(slot[0:1, :, 0:2], ALONG, -1)
        lower_y = shifted(slot[:, :, 6:8], "gy", 1)
        upper_y = shifted(slot[:, :, 4:6], "gy", -1)
        lower_x = jnp.concatenate([from_below, slot[0:1, :, 2:4]], 0)
        upper_x = jnp.concatenate([slot[1:2, :, 0:2], from_above], 0)
        facing = jnp.concatenate([lower_x, upper_x, lower_y, upper_y], 2)
        back = jnp.einsum("sqk,srqc->srkc", table, facing, precision=HI)
        return back.reshape(subs, rows, wide)

    def jump(field):
        return field - partner(field)

    def inner(left, right):
        return jnp.einsum("srk,stk->rt", left * wloc, right, precision=HI)

    def plain(left, right):
        return jnp.einsum("srk,stk->rt", left, right, precision=HI)

    def applied(field):
        return jnp.einsum("srk,skj->srj", field, dual, precision=HI)

    def combine(field, mixing):
        return jnp.einsum("srk,rt->stk", field, mixing, precision=HI)

    def mixed(alpha, mixing):
        return jnp.einsum("smr,rt->smt", alpha, mixing, precision=HI)

    def lifted(alpha, basis):
        return jnp.einsum("smr,smk->srk", alpha, basis, precision=HI)

    def collect(parts):
        parts = parts.reshape(2, 5, modes, parts.shape[-1])
        below = shifted(parts[1, 2], ALONG, 1)
        above = shifted(parts[0, 1], ALONG, -1)
        left = shifted(parts[:, 4], "gy", 1)
        right = shifted(parts[:, 3], "gy", -1)
        inside = jnp.stack([below + parts[1, 1], parts[0, 2] + above])
        return (parts[:, 0] + inside + left + right) * live

    load = (rigid_load[:, 0] * live).reshape(-1, 128)
    gathered = gather(load)
    wide = coarse_inverse.shape[-1]
    half = wide // 2
    quarter = half // 4
    rows = coarse_inverse.reshape(2 * modes, lax.axis_size("y"), 2, -1, 4)
    rows = rows.transpose(0, 2, 4, 1, 3).reshape(2, modes, wide) * live
    below = shifted(rows[1], ALONG, 1)
    above = shifted(rows[0], ALONG, -1)
    left = shifted(rows, "gy", 1)
    right = shifted(rows, "gy", -1)
    near = jnp.stack(
        [rows, jnp.stack([below, rows[0]]), jnp.stack([rows[1], above]), left, right], 1
    ).reshape(2, 5 * modes, wide)

    facing = partner(jnp.concatenate([trace, gap], 1))
    gap_jump = gap - facing[:, modes:]
    basis = jnp.concatenate(
        [trace] + [jnp.where(side[:, None, :] == d, -facing[:, :modes], 0.0) for d in range(4)], 1
    )
    pushed_basis = applied(basis)
    couple = jnp.einsum("smk,snk->smn", trace, basis, precision=HI) * live
    couple_rows = jnp.einsum("smn,snw->smw", couple, near, precision=HI)
    push = jnp.einsum("smk,snk->smn", basis, pushed_basis, precision=HI)
    push_rows = collect(jnp.einsum("smn,snw->smw", push, near, precision=HI))
    stack = jnp.concatenate(
        [part.reshape(-1, wide) for part in (near, push_rows, couple_rows)], 0
    )
    count = stack.shape[0]
    stack = stack.reshape(count, 2, half)
    mine = lax.dynamic_index_in_dim(stack, core, 1, keepdims=False)
    theirs = other_core(lax.dynamic_index_in_dim(stack, 1 - core, 1, keepdims=False))
    folded = jnp.stack([mine, theirs]).reshape(2 * count * 4, quarter)
    lane = jnp.arange(128, dtype=jnp.int32)[None, :] // cases
    keep = (lane == jnp.arange(4, dtype=jnp.int32)[:, None]).astype(jnp.float32)

    def coarse(gathered, sums=None):
        product = jnp.dot(folded, gathered, precision=HI).reshape(2, count, 4, 128)
        product = (product * keep).sum(2)
        away = product[1] if sums is None else jnp.concatenate([product[1], sums], 0)
        away = other_core(away)
        total = product[0] + away[:count]
        total = sum(total[:, q * cases : (q + 1) * cases] for q in range(4))
        near_alpha = total[: 10 * modes].reshape(2, 5 * modes, cases)
        rest = total[10 * modes :].reshape(2, 2, modes, cases)
        if sums is None:
            return near_alpha, rest[0], rest[1]
        return near_alpha, rest[0], rest[1], sums + away[count:]

    def loads(field):
        return jnp.einsum("smk,srk->smr", trace, field, precision=HI) * live

    def loads_of_jump(field):
        return collect(jnp.einsum("smk,srk->smr", basis, field, precision=HI))

    def packed(*grams):
        return jnp.concatenate([gram.reshape(-1, 128) for gram in grams], 0)

    alpha0, push0, _ = coarse(gathered)
    load_force = loads(gap_jump) - push0
    gathered = gather(load_force)
    first_solution = lifted(alpha0, basis)
    force = gap_jump - jump(lifted(alpha0, pushed_basis))
    push_force = applied(force)
    load_push_force = loads_of_jump(push_force)

    alpha1, push1, couple1 = coarse(gathered)
    load_resid = load_force - couple1
    gathered = gather(load_resid)
    resid = force - lifted(alpha1, basis)
    push_resid = push_force - lifted(alpha1, pushed_basis)
    load_push_resid = load_push_force - push1
    resid_gram = inner(resid, resid)

    alpha2, push2, _ = coarse(gathered)
    load_hit = load_push_resid - push2
    moved = resid - lifted(alpha2, basis)
    pushed = push_resid - lifted(alpha2, pushed_basis)
    gathered, sums = gather_and_sum(load_hit, packed(plain(moved, pushed), resid_gram))
    hit = jump(pushed)
    push_hit = applied(hit)
    load_push_hit = loads_of_jump(push_hit)

    alpha3, push3, couple3, sums = coarse(gathered, sums)
    curvature, drive = sums.reshape(2, cases, cases)
    load_image = load_hit - couple3
    image = hit - lifted(alpha3, basis)
    gathered, sums = gather_and_sum(load_image, packed(inner(image, image)))
    step = chol_solve(curvature, drive)
    push_image = push_hit - lifted(alpha3, pushed_basis)
    load_push_image = load_push_hit - push3
    next_resid = resid - combine(image, step)

    alpha_image, push_alpha_image, _, sums = coarse(gathered, sums)
    image_gram = sums.reshape(cases, cases)
    cross = curvature.T - jnp.dot(image_gram, step, precision=HI)
    coupling = chol_solve(curvature, cross)
    mix = jnp.eye(cases, dtype=jnp.float32) - coupling
    direction = next_resid - combine(resid, coupling)
    alpha4 = mixed(alpha2, mix) - mixed(alpha_image, step)
    push4 = mixed(push2, mix) - mixed(push_alpha_image, step)
    load_hit = mixed(load_push_resid, mix) - mixed(load_push_image, step) - push4
    next_moved = direction - lifted(alpha4, basis)
    pushed = combine(push_resid, mix) - combine(push_image, step) - lifted(alpha4, pushed_basis)
    gathered, sums = gather_and_sum(
        load_hit, packed(plain(next_moved, pushed), inner(direction, next_resid))
    )
    hit = jump(pushed)
    partial_solution = first_solution + combine(moved, step)

    alpha5, _, _, sums = coarse(gathered, sums)
    curvature, drive = sums.reshape(2, cases, cases)
    next_step = chol_solve(curvature, drive)
    image = hit - lifted(alpha5, basis)
    answer = partial_solution + combine(next_moved, next_step)
    return (answer[:, None], (next_resid - combine(image, next_step))[:, None])


def solution(mesh):
    along, across = mesh.devices.shape
    fine = Mesh(mesh.devices.reshape(along // 2, 2, across), ("y", "core", "gy"))
    wide = P(ALONG, "gy", None, None)
    return jax.shard_map(
        per_device,
        mesh=fine,
        in_specs=(wide, wide, wide, P(ALONG, "gy"), P(ALONG, "gy", None), wide, wide),
        out_specs=(wide, wide),
        check_vma=False,
    )
```

```python
import jax
import jax.numpy as jnp
from jax import lax
from jax.experimental import pallas as pl
from jax.experimental.pallas import tpu as pltpu
from jax.sharding import Mesh, PartitionSpec as P


HI = lax.Precision.HIGHEST
ALONG = ("y", "core")


def swapped(value, axis, start):
    count = lax.axis_size(axis)
    pairs = [(k, k + 1) for k in range(start, count - 1, 2)]
    return lax.ppermute(value, axis, pairs + [(k, j) for j, k in pairs])


def beside(down, up, axis):
    even = lax.axis_index(axis) % 2 == 0
    one = swapped(jnp.where(even, up, down), axis, 0)
    two = swapped(jnp.where(even, down, up), axis, 1)
    return jnp.where(even, two, one), jnp.where(even, one, two)


def other_core(value):
    return lax.ppermute(value, "core", [(0, 1), (1, 0)])


def slot_table(block_map):
    slots = jnp.arange(8, dtype=jnp.int32)
    return (block_map[..., None, :] == slots[:, None]).astype(jnp.float32)


def slot_weights(first, second, sx_all, sy_all):
    first_b, second_b = jnp.broadcast_arrays(first, second)
    outside = jnp.stack(
        [first_b == 0, first_b == sx_all - 1, second_b == 0, second_b == sy_all - 1], -1
    )
    outside = jnp.repeat(outside, 2, axis=-1)
    return jnp.where(outside, 1.0, 0.5).astype(jnp.float32)


def split(value):
    high = value.astype(jnp.bfloat16)
    return high, (value - high.astype(jnp.float32)).astype(jnp.bfloat16)


def dual_kernel(field_ref, dual_ref, out_ref):
    rows = field_ref.shape[1]
    high, low = split(field_ref[0])
    dual_high, dual_low = split(dual_ref[0])
    both = jnp.concatenate([high, low], 0)
    main = jnp.dot(both, dual_high, preferred_element_type=jnp.float32)
    rest = jnp.dot(high, dual_low, preferred_element_type=jnp.float32)
    part = main[:rows] + (main[rows:] + rest)

    @pl.when(pl.program_id(1) == 0)
    def _():
        out_ref[0] = part

    @pl.when(pl.program_id(1) > 0)
    def _():
        out_ref[0] += part


def dual_product(field, dual):
    subs, rows, width = field.shape
    block = min(width, 256)
    return pl.pallas_call(
        dual_kernel,
        grid=(subs, width // block),
        in_specs=[
            pl.BlockSpec((1, rows, block), lambda s, k: (s, 0, k)),
            pl.BlockSpec((1, block, width), lambda s, k: (s, k, 0)),
        ],
        out_specs=pl.BlockSpec((1, rows, width), lambda s, k: (s, 0, 0)),
        out_shape=jax.ShapeDtypeStruct(field.shape, jnp.float32),
        compiler_params=pltpu.CompilerParams(vmem_limit_bytes=24 * 1024 * 1024),
        cost_estimate=pl.CostEstimate(
            flops=6 * subs * rows * width * width,
            bytes_accessed=4 * subs * width * width,
            transcendentals=0,
        ),
    )(field, dual)


def invert(work):
    size = work.shape[0]
    row_of = lax.broadcasted_iota(jnp.int32, work.shape, 0)
    for base in range(0, size, 8):
        columns = [
            jnp.broadcast_to(work[:, j : j + 1], work.shape) for j in range(base, base + 8)
        ]
        for k in range(8):
            j, column = base + k, columns[k]
            scale = lax.rsqrt(column[j : j + 1])
            scale = scale * scale
            row = work[j : j + 1] * scale
            work = jnp.where(row_of == j, row, work - column * row)
            for m in range(k + 1, 8):
                row = columns[m][j : j + 1] * scale
                columns[m] = jnp.where(row_of == j, row, columns[m] - column * row)
    return work


def small_dot(left, right):
    return jnp.dot(left, right, precision=HI, preferred_element_type=jnp.float32)


def turned_dot(left, right):
    return lax.dot_general(
        left, right, (((0,), (0,)), ((), ())), precision=HI, preferred_element_type=jnp.float32
    )


def pack(gram):
    size = gram.shape[0] // 4
    return jnp.concatenate([gram[q * size : (q + 1) * size] for q in range(4)], 1)


def unpack(rows):
    size = rows.shape[1] // 4
    return jnp.concatenate([rows[:, q * size : (q + 1) * size] for q in range(4)], 0)


def middle_kernel(
    sums_ref, resid_ref, image_ref, alpha_ref, alpha_image_ref, basis_ref, weight_ref,
    step_ref, next_ref, moved_ref, drive_ref,
):
    curvature, drive, gram = (unpack(sums_ref[8 * q : 8 * q + 8]) for q in range(3))
    size = curvature.shape[0]
    turned = curvature.T
    row = lax.broadcasted_iota(jnp.int32, curvature.shape, 0)
    eye = (row == lax.broadcasted_iota(jnp.int32, curvature.shape, 1)).astype(jnp.float32)
    solved = invert(jnp.concatenate([0.5 * (curvature + turned), eye, drive, turned], 1))
    inverse, step = solved[:, size : 2 * size], solved[:, 2 * size : 3 * size]
    coupling = solved[:, 3 * size :] - small_dot(inverse, small_dot(gram, step))
    mix = eye - coupling
    step_ref[...] = step
    total = jnp.zeros_like(step)
    for s in range(2):
        resid = resid_ref[s]
        following = resid - turned_dot(step, image_ref[s])
        direction = following - turned_dot(coupling, resid)
        alpha = small_dot(alpha_ref[s], mix) - small_dot(alpha_image_ref[s], step)
        next_ref[s] = following
        moved_ref[s] = direction - turned_dot(alpha, basis_ref[s])
        total += lax.dot_general(
            direction * weight_ref[s], following, (((1,), (1,)), ((), ())),
            precision=HI, preferred_element_type=jnp.float32,
        )
    drive_ref[...] = total


def end_kernel(
    sums_ref, first_ref, moved_ref, next_moved_ref, hit_ref, resid_ref, alpha_ref, basis_ref,
    step_ref, answer_ref, out_ref,
):
    curvature, drive = (unpack(sums_ref[8 * q : 8 * q + 8]) for q in range(2))
    size = curvature.shape[0]
    solved = invert(jnp.concatenate([0.5 * (curvature + curvature.T), drive], 1))
    step, next_step = step_ref[...], solved[:, size:]
    for s in range(2):
        answer = first_ref[s] + turned_dot(step, moved_ref[s])
        answer_ref[s] = answer + turned_dot(next_step, next_moved_ref[s])
        image = hit_ref[s] - turned_dot(alpha_ref[s], basis_ref[s])
        out_ref[s] = resid_ref[s] - turned_dot(next_step, image)


def whole_call(kernel, shapes, *arrays):
    return pl.pallas_call(
        kernel,
        out_shape=[jax.ShapeDtypeStruct(shape, jnp.float32) for shape in shapes],
        compiler_params=pltpu.CompilerParams(vmem_limit_bytes=32 * 1024 * 1024),
    )(*arrays)


def spread_out(value, axis):
    count = lax.axis_size(axis)
    copies = jnp.broadcast_to(value, (count,) + value.shape)
    return lax.all_to_all(copies, axis, 0, 0, tiled=False)


def gather(rows):
    return spread_out(rows.reshape(1, -1), ("y", "gy")).reshape(-1, 128)


def gather_and_sum(rows, sums):
    rows = rows.reshape(-1, 128)
    count = rows.shape[0]
    both = spread_out(jnp.concatenate([rows, sums], 0), "gy")
    part = both[:, :count].reshape(-1, 128)
    both = jnp.concatenate([part, both[:, count:].sum(0)], 0)
    size = lax.axis_size("y")
    place = lax.axis_index("y")
    blocks = [both] + [
        lax.ppermute(both, "y", [(i, i ^ s) for i in range(size)]) for s in range(1, size)
    ]
    total = sum(block[part.shape[0] :] for block in blocks)
    blocks = [block[: part.shape[0]] for block in blocks]
    bit = 1
    while bit < size:
        blocks = [jnp.where(place & bit, blocks[j ^ bit], blocks[j]) for j in range(size)]
        bit *= 2
    return jnp.concatenate(blocks, 0), total


def per_device(
    dual_operators, rigid_trace, coarse_inverse, floating, block_map, interface_gap, rigid_load
):
    count_x = lax.axis_size("y") * lax.axis_size("core")
    count_y = lax.axis_size("gy")
    core = lax.axis_index("core")
    place_x = lax.axis_index("y") * lax.axis_size("core") + core
    place_y = lax.axis_index("gy")
    dual = dual_operators[:, 0]
    trace = rigid_trace[:, 0]
    gap = interface_gap[:, 0]
    modes, width = trace.shape[1:]
    cases = gap.shape[1]
    table = slot_table(block_map[:, 0])
    first = 2 * place_x + jnp.arange(2, dtype=jnp.int32)[:, None]
    second = jnp.full((1, 1), place_y, jnp.int32)
    omega = slot_weights(first, second, 2 * count_x, count_y)[:, 0]
    wblock = jnp.einsum("sqk,sq->sk", table, omega, precision=HI)
    wloc = jnp.repeat(wblock, width // 8, axis=-1)[:, None, :]
    side = jnp.repeat(block_map[:, 0] // 2, width // 8, axis=-1)
    live = floating[:, 0].astype(jnp.float32)[:, None, None]

    def slots_of(field):
        subs, rows, wide = field.shape
        blocks = field.reshape(subs, rows, 8, wide // 8)
        return jnp.einsum("sqk,srkc->srqc", table, blocks, precision=HI)

    def dofs_of(slot):
        back = jnp.einsum("sqk,srqc->srkc", table, slot, precision=HI)
        return back.reshape(back.shape[:2] + (-1,))

    def faced(slot, below, above, left, right):
        lower = jnp.concatenate([below, slot[0:1, :, 2:4]], 0)
        upper = jnp.concatenate([slot[1:2, :, 0:2], above], 0)
        return dofs_of(jnp.concatenate([lower, upper, left, right], 2))

    def partner(field):
        slot = slots_of(field)
        down, up = slot[0:1, :, 0:2], slot[1:2, :, 2:4]
        back, ahead = slot[:, :, 4:6], slot[:, :, 6:8]
        outside = swapped(jnp.where(core == 0, down, up), ALONG, 1)
        got = other_core(
            jnp.concatenate([jnp.where(core == 0, up, down), jnp.where(core == 0, back, ahead)], 0)
        )
        inside, theirs = got[:1], got[1:]
        size = lax.axis_size("gy")
        pairs = [(k, size + k + 1) for k in range(size - 1)]
        across = lax.ppermute(
            jnp.where(core == 0, jnp.stack([ahead, theirs]), jnp.stack([theirs, back])),
            ("core", "gy"),
            pairs + [(k, j) for j, k in pairs],
        )
        kept = jnp.where(core == 0, across[0], across[1])
        got = other_core(jnp.where(core == 0, across[1], across[0]))
        left = jnp.where(core == 0, got, kept)
        right = jnp.where(core == 0, kept, got)
        below = jnp.where(core == 0, outside, inside)
        above = jnp.where(core == 0, inside, outside)
        return faced(slot, below, above, left, right)

    def jump(field):
        return field - partner(field)

    def inner(left, right):
        return jnp.einsum("srk,stk->rt", left * wloc, right, precision=HI)

    def plain(left, right):
        return jnp.einsum("srk,stk->rt", left, right, precision=HI)

    def applied(field):
        return dual_product(field, dual)

    def combine(field, mixing):
        return jnp.einsum("srk,rt->stk", field, mixing, precision=HI)

    def mixed(alpha, mixing):
        return jnp.einsum("smr,rt->smt", alpha, mixing, precision=HI)

    def lifted(alpha, basis):
        return jnp.einsum("smr,smk->srk", alpha, basis, precision=HI)

    load = (rigid_load[:, 0] * live).reshape(-1, 128)
    gathered = gather(load)
    half = coarse_inverse.shape[-1] // 2
    rows = coarse_inverse.reshape(2 * modes, lax.axis_size("y"), 2, -1, 4)
    rows = rows.transpose(2, 0, 4, 1, 3).reshape(2, 2, modes, half) * live
    part = width // 8
    slot = jnp.einsum(
        "sqk,smkc->sqmc", table, trace.reshape(2, modes, 8, part), precision=HI
    )
    slot = lax.optimization_barrier(slot)
    edges = jnp.concatenate([slot[:, q] for q in range(4)], -1)
    mine = lax.dynamic_index_in_dim(rows, core, 0, keepdims=False)
    theirs = lax.dynamic_index_in_dim(rows, 1 - core, 0, keepdims=False)
    mine = jnp.concatenate([mine, edges], -1)
    theirs = other_core(jnp.concatenate([theirs, edges], -1))
    chip = jnp.concatenate(
        [jnp.where(core == 0, mine, theirs), jnp.where(core == 0, theirs, mine)], 0
    )
    below, above = beside(chip[0], chip[3], "y")
    flat = chip[..., :half].reshape(4 * modes, half)
    down, up = (
        jnp.concatenate([flat, slot[:, q : q + 2].reshape(4 * modes, part)], -1) for q in (4, 6)
    )
    left, right = beside(down, up, "gy")
    stack = jnp.concatenate(
        [below[:, :half], flat, above[:, :half], left[:, :half], right[:, :half]], 0
    )
    count = stack.shape[0]
    folded = stack.reshape(count * 4, half // 4)
    lane = jnp.arange(128, dtype=jnp.int32)[None, :] // cases
    keep = (lane == jnp.arange(4, dtype=jnp.int32)[:, None]).astype(jnp.float32)
    below = jnp.where(core == 0, below, theirs[1])[:, half:]
    above = jnp.where(core == 0, theirs[0], above)[:, half:]
    below = jnp.stack([below[:, q * part : (q + 1) * part] for q in (2, 3)])[None]
    above = jnp.stack([above[:, q * part : (q + 1) * part] for q in (0, 1)])[None]
    facing = jnp.concatenate(
        [
            jnp.concatenate([below, slot[0:1, 2:4]], 0),
            jnp.concatenate([slot[1:2, 0:2], above], 0),
            left[:, half:].reshape(2, 2, modes, part),
            right[:, half:].reshape(2, 2, modes, part),
        ],
        1,
    )
    facing = jnp.einsum("sqk,sqmc->smkc", table, facing, precision=HI).reshape(2, modes, width)
    basis = jnp.concatenate(
        [trace] + [jnp.where(side[:, None, :] == d, -facing, 0.0) for d in range(4)], 1
    )

    def coarse(gathered, sums=None):
        product = jnp.dot(folded, gathered, precision=HI).reshape(count, 4, 128)
        product = (product * keep).sum(1)
        if sums is not None:
            product = jnp.concatenate([sums, product], 0)
        total = product + other_core(product)
        added = total.shape[0] - count
        alpha = total[added:].reshape(14, modes, 128)
        alpha = sum(alpha[..., q * cases : (q + 1) * cases] for q in range(4))
        line = jnp.where(core == 0, alpha[0:4], alpha[2:6])
        left = jnp.where(core == 0, alpha[6:8], alpha[8:10])
        right = jnp.where(core == 0, alpha[10:12], alpha[12:14])
        near = jnp.stack([line[1:3], line[0:2], line[2:4], left, right], 1)
        near = near.reshape(2, 5 * modes, cases)
        return near if sums is None else (near, total[:added])

    def loads(field):
        return jnp.einsum("smk,srk->smr", trace, field, precision=HI) * live

    def packed(*grams):
        return jnp.concatenate([pack(gram) for gram in grams], 0)

    first_solution = lifted(coarse(gathered), basis)
    force = jump(gap - applied(first_solution))
    resid = force - lifted(coarse(gather(loads(force))), basis)
    alpha = coarse(gather(loads(resid)))
    moved = resid - lifted(alpha, basis)
    pushed = applied(moved)
    hit = jump(pushed)
    image = hit - lifted(coarse(gather(loads(hit))), basis)
    gathered, sums = gather_and_sum(
        loads(image), packed(plain(moved, pushed), inner(resid, resid), inner(image, image))
    )
    alpha_image, sums = coarse(gathered, sums)
    square = (cases, cases)
    step, next_resid, next_moved, drive = whole_call(
        middle_kernel,
        [square, resid.shape, resid.shape, square],
        sums, resid, image, alpha, alpha_image, basis, wloc,
    )
    pushed = applied(next_moved)
    hit = jump(pushed)
    gathered, sums = gather_and_sum(
        loads(hit), packed(plain(next_moved, pushed), drive)
    )
    alpha, sums = coarse(gathered, sums)
    answer, last_resid = whole_call(
        end_kernel,
        [resid.shape, resid.shape],
        sums, first_solution, moved, next_moved, hit, next_resid, alpha, basis, step,
    )
    return (answer[:, None], last_resid[:, None])


def solution(mesh):
    along, across = mesh.devices.shape
    fine = Mesh(mesh.devices.reshape(along // 2, 2, across), ("y", "core", "gy"))
    wide = P(ALONG, "gy", None, None)
    return jax.shard_map(
        per_device,
        mesh=fine,
        in_specs=(wide, wide, wide, P(ALONG, "gy"), P(ALONG, "gy", None), wide, wide),
        out_specs=(wide, wide),
        check_vma=False,
    )
```
